32 devices in a mesh: seq: 4 (over y, core), exp: 4 (over z), rep: 2 (over x).
Axes of the slice: x: 2, y: 2, z: 4, core: 2. Of those that a mesh axis runs over, the one named last changes fastest.
Arguments:
- queries: bfloat16 [512, 6144], P('seq'), may hold values from -80 to 80
- keys: bfloat16 [512, 1024], P('seq'), may hold values from -4.2 to 4.2
- values: bfloat16 [512, 1024], P('seq'), may hold values from -6.2 to 6.2
- lengths: int32 [4], replicated, may hold values from 1 to 256, 512 in all
- expert_ids: int32 [512, 4], P('seq'), may hold values from 0 to 15, all different within a row; in each aligned block of 128 rows (0 to 127, 128 to 255, ...) at most 34 rows name the same one
- gate_share: float32 [512, 4], P('seq'), may hold values from 0.2 to 1
- gate_up: bfloat16 [16, 6144, 2, 5376], P('exp', 'rep', None, 'seq'), may hold values from -0.15625 to 0.15625
- down_t: bfloat16 [16, 6144, 5376], P('exp', 'rep', 'seq'), may hold values from -0.15625 to 0.15625
Outputs:
- moe_out: bfloat16 [512, 6144], P(('seq', 'exp'), 'rep')
The draws below stay inside these ranges and needn't reach their ends.
Inputs may be any that keep to these rules, and one draw needn't show every extreme that they name: The lengths sum to 512; each is at most 256, and one is exactly 256. `expert_ids`: each token names 4 different experts. Among the 128 tokens of one device (aligned blocks of 128 positions), no expert is named more than 34 times, a bound that some block reaches.
All inputs are finite; a program needn't handle non-finite values.
Results may differ from the reference program's by a relative error of at most 0.035.
Values may be sent and summed in bfloat16 or wider, within the bound.
A program may use at most 192 MiB of HBM per device.

```python
import math
import jax
import jax.numpy as jnp
import numpy as np
from jax import lax

HEADS = 48
KV = 8
HD = 128
EXPERTS = 16
TOPK = 4
FFW = 5376
TOK_DEV = 128
REACH = 2
DOC_MOST = 256
D = 6144
L = 512
DOCS = 4
CAP = 34
N_SEQ = 4
N_EXP = 4
N_REP = 2


def drawn_keys(key):
    first = jax.random.fold_in(key, 0)
    rows = jnp.clip(jax.random.normal(first, (L, KV, HD), jnp.float32), -4.0, 4.0)
    return rows


def draw_keys(key, part):
    rows = drawn_keys(key)
    return rows.reshape(L, KV * HD).astype(jnp.bfloat16)


def draw_queries(key, part):
    key = jax.random.fold_in(key, 5)
    base = jnp.clip(jax.random.normal(key, (L, KV, HEADS // KV, HD), jnp.float32), -4.0, 4.0)
    return base.reshape(L, HEADS * HD).astype(jnp.bfloat16)


def draw_values(key, part):
    key = jax.random.fold_in(key, 17)
    first, second = jax.random.split(key, 2)
    common = 0.7 * jnp.clip(jax.random.normal(first, (KV * HD,), jnp.float32), -3.0, 3.0)
    noise = jnp.clip(jax.random.normal(second, (L, KV * HD), jnp.float32), -4.0, 4.0)
    return (common[None, :] + noise).astype(jnp.bfloat16)


def shard_levels(key, extent, pieces, smallest, high):
    level, own = 1.0, jax.random.fold_in(key, 6)
    for axis_at, blocks in pieces:
        steps = jnp.exp(jax.random.uniform(jax.random.fold_in(own, axis_at), (blocks,), jnp.float32, smallest / len(pieces), high / len(pieces)))
        level = level * jnp.repeat(steps, extent[axis_at] // blocks).reshape([-1 if axis == axis_at else 1 for axis in range(len(extent))])
    return level


def split_up(count, total, limit, skew):
    portions = [(1 << 20) // math.isqrt(grade ** skew) + 1 for grade in range(2, count + 1)]
    rest, holding = total - limit - (count - 1), [1] * (count - 1)
    while rest > 0:
        candidates = [i for i in range(count - 1) if holding[i] < limit]
        whole, left = sum([portions[i] for i in candidates]), rest
        for i in candidates:
            extra = min(limit - holding[i], max(1, left * portions[i] // whole), rest)
            holding[i] = holding[i] + extra
            rest = rest - extra
    return np.array([limit] + holding)


def ragged_sizes(stream_key, number_of, total, reach, slope):
    if number_of == 2:
        one = jax.random.randint(stream_key, (), max(1, total - reach), min(reach, total - 1) + 1)
        return jnp.stack([one, total - one])
    sizes = jnp.asarray(split_up(number_of, total, reach, slope), jnp.int32)
    twos = (number_of - 1) // 2
    source_of, receiver = sizes[1:1 + 2 * twos:2], sizes[2:2 + 2 * twos:2]
    margin = jnp.minimum(source_of - 1, reach - receiver)
    shifted = jax.random.randint(jax.random.fold_in(stream_key, 1), (twos,), 0, 1 << 20) % (margin + 1)
    sizes = sizes.at[1:1 + 2 * twos:2].set(source_of - shifted).at[2:2 + 2 * twos:2].set(receiver + shifted)
    return sizes[jax.random.permutation(jax.random.fold_in(stream_key, 2), number_of)]


def routed_block(key, own, number, rows, amount, top, most, slope):
    ranking = jax.random.permutation(key, amount)
    packed, usual = portions_of(amount, rows * top, most, slope, True), portions_of(amount, rows * top, most, slope, False)
    places = jnp.arange(amount)

    def named(tallies, turn):
        used = int((tallies > 0).sum())
        fixed = max(1, used // 4)
        moved = fixed + (places - fixed + turn * (used - fixed)) % max(1, amount - fixed)
        return jnp.zeros((amount,), jnp.int32).at[ranking[jnp.where(places < fixed, places, moved)]].set(jnp.asarray(tallies, jnp.int32))

    tallies = jnp.where(number % 4 == 0, named(packed, number // 4), named(usual, number - number // 4 - 1))
    mixed = jax.random.permutation(jax.random.fold_in(own, 3), amount)
    giver, receiver = mixed[0:amount // 2 * 2:2], mixed[1:amount // 2 * 2:2]
    room = jnp.minimum(tallies[giver] - 1, most - tallies[receiver]) // 2
    room = jnp.where((giver == ranking[0]) | (receiver == ranking[0]) | (tallies[receiver] == 0), 0, jnp.maximum(room, 0))
    moved = jax.random.randint(jax.random.fold_in(own, 4), (amount // 2,), 0, 1 << 20) % (room + 1)
    tallies = tallies.at[giver].add(-moved).at[receiver].add(moved)
    items = jnp.searchsorted(jnp.cumsum(tallies), jnp.arange(rows * top), side="right").astype(jnp.int32)
    table = items.reshape(top, rows).T
    table = table[jax.random.permutation(jax.random.fold_in(own, 1), rows)]
    turn = jax.random.randint(jax.random.fold_in(own, 2), (rows, 1), 0, top)
    return jnp.take_along_axis(table, (jnp.arange(top)[None, :] + turn) % top, axis=1)


def portions_of(number_of, total, most, lean, full):
    portions = [(1 << 20) // math.isqrt(standing ** lean) + 1 for standing in range(1, number_of + 1)]
    largest = most if full else min(most, max(-(-total // number_of), total * portions[0] // sum(portions)))
    least = 1 if total - largest >= number_of - 1 else 0
    given, spare = [largest] + [least] * (number_of - 1), total - largest - least * (number_of - 1)
    while spare > 0:
        movable = [i for i in range(1, number_of) if given[i] < largest] or [i for i in range(1, number_of) if given[i] < most]
        whole, budget = sum([portions[i] for i in movable]), spare
        for i in movable:
            more = min(most - given[i], max(1, budget * portions[i] // whole), spare)
            given[i] = given[i] + more
            spare = spare - more
    return np.array(given)


def gaussian(key, shape, scale, limit, cuts=(), held_as=jnp.bfloat16):
    array = jax.random.normal(key, shape, jnp.float32) * scale
    if len(cuts) > 0:
        array = shard_levels(key, shape, cuts, -0.22, 0.18) * array
    return jnp.clip(array, min=-limit, max=limit).astype(held_as)


def setup_inputs(seed: int = 0) -> dict:
    seeds = jax.random.split(jax.random.key(seed), 9)
    queries = draw_queries(jax.random.fold_in(seeds[8], 71), 0)
    keys = draw_keys(jax.random.fold_in(seeds[8], 71), 0)
    values = draw_values(jax.random.fold_in(seeds[8], 71), 0)
    lengths = ragged_sizes(seeds[3], DOCS, L, DOC_MOST, 2).astype(jnp.int32)
    expert_ids_keys = jax.random.split(jax.random.fold_in(seeds[4], 1), L // TOK_DEV)
    expert_ids_turns = jax.random.permutation(jax.random.fold_in(seeds[4], 3), L // TOK_DEV)
    expert_ids = jax.vmap(lambda own, number: routed_block(jax.random.fold_in(seeds[4], 2), own, number, TOK_DEV, EXPERTS, TOPK, CAP, 2))(expert_ids_keys, expert_ids_turns).reshape((L, TOPK))
    gate_share = jnp.clip(0.2 + 0.8 * jax.random.uniform(seeds[5], (L, TOPK), jnp.float32) ** shard_levels(seeds[5], (L, TOPK), ((0, 4),), -0.2, 0.2), 0.2, 1.0)
    gate_up = gaussian(seeds[6], (EXPERTS, D, 2, FFW), (D // 4) ** -0.5, 0.15625, ((0, 4), (1, 2), (3, 4)))
    down_t = gaussian(seeds[7], (EXPERTS, D, FFW), (FFW // 4) ** -0.5, 0.15625, ((0, 4), (1, 2), (2, 4)))
    return {"queries": queries, "keys": keys, "values": values, "lengths": lengths, "expert_ids": expert_ids, "gate_share": gate_share, "gate_up": gate_up, "down_t": down_t}


def segment_ids(lens, length):
    ends = jnp.cumsum(lens).astype(jnp.int32)
    places = jnp.arange(length, dtype=jnp.int32)
    return jnp.sum((places[:, None] >= ends[None, :]).astype(jnp.int32), axis=1)


def earlier(blocks_arr, back, fill):
    padding = jnp.full((back,) + blocks_arr.shape[1:], fill, blocks_arr.dtype)
    return jnp.concatenate([padding, blocks_arr[:blocks_arr.shape[0] - back]], 0)


def widen(blocks_arr, fill):
    parts = [earlier(blocks_arr, back, fill) for back in range(REACH, 0, -1)]
    return jnp.concatenate(parts + [blocks_arr], 1)


def attend(query, key_rows, value_rows, lens):
    segment = segment_ids(lens, L)
    tiles = L // TOK_DEV
    group = HEADS // KV
    q_tile = query.reshape(tiles, TOK_DEV, KV, group, HD).astype(jnp.float32)
    k_wide = widen(key_rows.reshape(tiles, TOK_DEV, KV, HD).astype(jnp.float32), 0.0)
    v_wide = widen(value_rows.reshape(tiles, TOK_DEV, KV, HD).astype(jnp.float32), 0.0)
    seg_tile = segment.reshape(tiles, TOK_DEV)
    seg_keys = widen(seg_tile, -1)
    q_pos = jnp.arange(L, dtype=jnp.int32).reshape(tiles, TOK_DEV)
    k_pos = q_pos[:, :1] - REACH * TOK_DEV + jnp.arange((REACH + 1) * TOK_DEV, dtype=jnp.int32)[None, :]
    allowed = (seg_tile[:, :, None] == seg_keys[:, None, :]) & (k_pos[:, None, :] <= q_pos[:, :, None])
    scores = jnp.einsum("ntsjd,nksd->nsjtk", q_tile, k_wide) * (HD ** -0.5)
    scores = jnp.where(allowed[:, None, None], scores, -jnp.inf)
    top = jnp.max(scores, axis=-1, keepdims=True)
    weights = jnp.exp(scores - top)
    probs = (weights / jnp.sum(weights, axis=-1, keepdims=True)).astype(jnp.bfloat16)
    out = jnp.einsum("nsjtk,nksd->ntsjd", probs.astype(jnp.float32), v_wide)
    return out.astype(jnp.bfloat16).reshape(L, HEADS * HD)


def one_expert(padded, index, shares, w_gate_up, w_down):
    rows = N_SEQ * CAP
    taken = padded[index].astype(jnp.float32).reshape(rows, N_REP, D // N_REP)
    weight = w_gate_up.astype(jnp.float32).reshape(N_REP, D // N_REP, 2 * FFW)
    parts = jnp.einsum("rbd,bdf->brf", taken, weight)
    parts = lax.optimization_barrier(parts.astype(jnp.bfloat16)).astype(jnp.float32)
    both = jnp.sum(parts, axis=0)
    hidden = (jax.nn.silu(both[:, :FFW]) * both[:, FFW:]).astype(jnp.bfloat16)
    hid = hidden.astype(jnp.float32).reshape(rows, N_SEQ, FFW // N_SEQ)
    down = w_down.astype(jnp.float32).reshape(D, N_SEQ, FFW // N_SEQ)
    outs = jnp.einsum("rsf,dsf->srd", hid, down)
    outs = lax.optimization_barrier(outs.astype(jnp.bfloat16)).astype(jnp.float32)
    expert_out = jnp.sum(outs, axis=0)
    return jnp.zeros((L + 1, D), jnp.float32).at[index].add(shares[:, None] * expert_out)


def reference(queries, keys, values, lengths, expert_ids, gate_share, gate_up, down_t):
    attended = attend(queries, keys, values, lengths)
    blocks = L // TOK_DEV
    ids = expert_ids.reshape(blocks, TOK_DEV * TOPK)
    onehot = (ids[:, :, None] == jnp.arange(EXPERTS, dtype=jnp.int32)[None, None, :]).astype(jnp.int32)
    before = (jnp.cumsum(onehot, axis=1) - onehot).astype(jnp.int32)
    slot = jnp.sum(before * onehot, axis=2).astype(jnp.int32)
    block_of = jnp.arange(blocks, dtype=jnp.int32)[:, None]
    dest = (ids * (blocks * CAP) + block_of * CAP + slot).reshape(-1).astype(jnp.int32)
    token_of = (jnp.arange(L * TOPK, dtype=jnp.int32) // TOPK).astype(jnp.int32)
    inverse = jnp.full((EXPERTS * blocks * CAP,), L, jnp.int32).at[dest].set(token_of)
    share_at = jnp.zeros((EXPERTS * blocks * CAP,), jnp.float32).at[dest].set(gate_share.reshape(-1))
    own = EXPERTS // N_EXP
    inverse = inverse.reshape(N_EXP, own, blocks * CAP)
    share_at = share_at.reshape(N_EXP, own, blocks * CAP)
    w_gate_up = gate_up.reshape(N_EXP, own, D, 2 * FFW)
    w_down = down_t.reshape(N_EXP, own, D, FFW)
    padded = jnp.concatenate([attended, jnp.zeros((1, D), jnp.bfloat16)], 0)

    def one_owner(total, inputs):
        index, shares, weight_a, weight_b = inputs
        term = jnp.zeros((L + 1, D), jnp.float32)
        for member in range(own):
            term = term + one_expert(padded, index[member], shares[member], weight_a[member], weight_b[member])
        term = lax.optimization_barrier(term[:L].astype(jnp.bfloat16)).astype(jnp.float32)
        return total + term, None

    total = jnp.zeros((L, D), jnp.float32)
    total, _ = lax.scan(one_owner, total, (inverse, share_at, w_gate_up, w_down))
    return total.astype(jnp.bfloat16)
```

```python
import jax
import jax.numpy as jnp
from jax import lax
from jax.sharding import PartitionSpec as P

HEADS = 48
KV = 8
HD = 128
TOPK = 4
REACH = 2
CAP = 34
GROUP = HEADS // KV
TAIL_PIECES = 2


def swap(x, axis, distance):
    n = lax.axis_size(axis)
    return lax.ppermute(x, axis, [(i, i ^ distance) for i in range(n)])


def shift(x, axis, distance):
    n = lax.axis_size(axis)
    return lax.ppermute(x, axis, [(i, i + distance) for i in range(n - distance)])


def bits_down(n):
    return [1 << b for b in reversed(range(n.bit_length() - 1))]


def gather_swapped(x, axis):
    n = lax.axis_size(axis)
    x = x[None]
    for bit in bits_down(n):
        other = swap(x, axis, bit)
        size = x.shape[0]
        both = jnp.stack([x, other], 1)
        x = both.reshape((2 * size,) + x.shape[1:]) if size > 1 else both[0]
    return x


def attend(queries, keys, values, lengths, kv_here, split):
    tok = queries.shape[0]
    s = lax.axis_index("seq")
    e = lax.axis_index("exp")
    r = lax.axis_index("rep")
    n_exp = lax.axis_size("exp")
    per = max(1, kv_here // n_exp)
    rows = tok // split
    head = r * kv_here + (e // split) * per
    k = lax.dynamic_slice_in_dim(keys, head * HD, per * HD, 1)
    v = lax.dynamic_slice_in_dim(values, head * HD, per * HD, 1)
    kv = jnp.concatenate([k, v], axis=1)
    wide = [shift(kv, "seq", back) for back in range(REACH, 0, -1)] + [kv]
    wide = jnp.concatenate(wide, 0)
    span = (REACH + 1) * tok
    k_wide = wide[:, : per * HD].reshape(span, per, HD)
    v_wide = wide[:, per * HD :].reshape(span, per, HD)
    q = lax.dynamic_slice(
        queries, ((e % split) * rows, head * GROUP * HD), (rows, per * GROUP * HD)
    ).reshape(rows, per, GROUP, HD)
    ends = jnp.cumsum(lengths)
    q_pos = s * tok + (e % split) * rows + jnp.arange(rows, dtype=jnp.int32)
    k_pos = (s - REACH) * tok + jnp.arange(span, dtype=jnp.int32)
    q_seg = jnp.sum((q_pos[:, None] >= ends[None, :]).astype(jnp.int32), axis=1)
    k_seg = jnp.sum((k_pos[:, None] >= ends[None, :]).astype(jnp.int32), axis=1)
    allowed = (
        (q_seg[:, None] == k_seg[None, :])
        & (k_pos[None, :] <= q_pos[:, None])
        & (k_pos[None, :] >= 0)
    )
    scores = jnp.einsum(
        "tpjd,kpd->pjtk", q, k_wide, preferred_element_type=jnp.float32
    ) * HD ** (-0.5)
    scores = jnp.where(allowed[None, None], scores, -jnp.inf)
    top = jnp.max(scores, axis=-1, keepdims=True)
    weights = jnp.exp(scores - top)
    probs = (weights / jnp.sum(weights, axis=-1, keepdims=True)).astype(jnp.bfloat16)
    out = jnp.einsum("pjtk,kpd->tpjd", probs, v_wide, preferred_element_type=jnp.float32)
    return out.astype(jnp.bfloat16).reshape(rows, per * GROUP * HD)


def gather_tokens(own, tok, cols, split):
    n_seq = lax.axis_size("seq")
    n_exp = lax.axis_size("exp")
    e = lax.axis_index("exp")
    rows, width = own.shape
    pieces = [own] + [swap(own, "exp", d) for d in range(1, n_exp)]
    bunch = max(1, n_exp // 4)
    full = jnp.zeros((n_seq, tok, cols), jnp.bfloat16)
    for first in range(0, n_exp, bunch):
        held = jnp.stack(pieces[first : first + bunch])
        got = gather_swapped(held, "seq")
        for j in range(bunch):
            at = e ^ (first + j)
            full = lax.dynamic_update_slice(
                full, got[:, j], (0, (at % split) * rows, (at // split) * width)
            )
    return full.reshape(n_seq * tok, cols)


def per_device(queries, keys, values, lengths, expert_ids, gate_share, gate_up, down_t):
    n_seq = lax.axis_size("seq")
    n_exp = lax.axis_size("exp")
    n_rep = lax.axis_size("rep")
    tok = queries.shape[0]
    owned, cols = gate_up.shape[0], gate_up.shape[1]
    e = lax.axis_index("exp")
    r = lax.axis_index("rep")
    kv_here = cols // (GROUP * HD)
    split = max(1, n_exp // kv_here)

    table = jnp.concatenate([expert_ids.astype(jnp.float32).T, gate_share.T], 0)
    table = gather_swapped(table, "seq")
    ids = table[:, :TOPK].astype(jnp.int32)
    shares = table[:, TOPK:]
    mine = e * owned + jnp.arange(owned, dtype=jnp.int32)
    hit = ids[None] == mine[:, None, None, None]
    match = jnp.any(hit, axis=2)
    share = jnp.sum(jnp.where(hit, shares[None], 0.0), axis=2)
    count = match.astype(jnp.int32)
    rank = jnp.cumsum(count, axis=2) - count
    block = jnp.arange(n_seq, dtype=jnp.int32)[None, :, None]
    key = jnp.where(match, block * CAP + rank, -1)
    rows = n_seq * CAP
    part = rows // n_rep
    at = jnp.arange(rows, dtype=jnp.int32)
    slot = (r ^ (at // part)) * part + at % part
    pick = (key.reshape(owned, 1, n_seq * tok) == slot[None, :, None]).astype(jnp.bfloat16)

    def turned(x):
        cut = x.reshape(owned, n_seq, n_exp, tok // n_exp)
        order = e ^ jnp.arange(n_exp, dtype=jnp.int32)
        return jnp.take(cut, order, axis=2).reshape(owned, n_seq * tok)

    key_out, share_out = turned(key), turned(share)
    spread = jnp.where(
        key_out.T[:, :, None] == slot[None, None, :], share_out.T[:, :, None], 0.0
    ).astype(jnp.bfloat16).reshape(n_seq * tok, owned * rows)

    own = attend(queries, keys, values, lengths, kv_here, split)
    tokens = gather_tokens(own, tok, cols, split)

    outs = []
    for i in range(owned):
        picked = jnp.dot(pick[i], tokens, preferred_element_type=jnp.float32).astype(jnp.bfloat16)
        both = jnp.einsum("rd,dgf->grf", picked, gate_up[i], preferred_element_type=jnp.float32)
        both = both.astype(jnp.bfloat16)
        total = both[:, :part].astype(jnp.float32)
        for d in range(1, n_rep):
            got = swap(both[:, d * part : (d + 1) * part], "rep", d)
            total = total + got.astype(jnp.float32)
        hidden = (jax.nn.silu(total[0]) * total[1]).astype(jnp.bfloat16)
        hidden = jnp.concatenate([hidden] + [swap(hidden, "rep", d) for d in range(1, n_rep)], 0)
        down = jnp.einsum("rf,df->rd", hidden, down_t[i], preferred_element_type=jnp.float32)
        outs.append(down.astype(jnp.bfloat16))
    outs = jnp.concatenate(outs, 0)

    results = []
    wide = cols // TAIL_PIECES
    for c in range(TAIL_PIECES):
        term = jnp.dot(
            spread, outs[:, c * wide : (c + 1) * wide], preferred_element_type=jnp.float32
        ).astype(jnp.bfloat16).reshape(n_seq, tok, wide)
        for bit in reversed(bits_down(n_seq)):
            pairs = term.reshape(term.shape[0] // 2, 2, tok, wide)
            got = swap(pairs[:, 1], "seq", bit)
            term = (pairs[:, 0].astype(jnp.float32) + got.astype(jnp.float32)).astype(jnp.bfloat16)
        chunks = term.reshape(n_exp, tok // n_exp, wide)
        total = chunks[0].astype(jnp.float32)
        for d in range(1, n_exp):
            total = total + swap(chunks[d], "exp", d).astype(jnp.float32)
        results.append(total.astype(jnp.bfloat16))
    return jnp.concatenate(results, 1)


def solution(mesh):
    in_specs = (
        P("seq", None),
        P("seq", None),
        P("seq", None),
        P(),
        P("seq", None),
        P("seq", None),
        P("exp", "rep", None, "seq"),
        P("exp", "rep", "seq"),
    )
    out_specs = P(("seq", "exp"), "rep")
    return jax.shard_map(
        per_device, mesh=mesh, in_specs=in_specs, out_specs=out_specs, check_vma=False
    )
```

```python
import jax
import jax.numpy as jnp
from jax import lax
from jax.experimental import pallas as pl
from jax.experimental.pallas import tpu as pltpu
from jax.sharding import PartitionSpec as P

HEADS = 48
KV = 8
HD = 128
TOPK = 4
REACH = 2
CAP = 34
GROUP = HEADS // KV
TAIL_PIECES = 2
SLOTS = 4
F_STEP = 384
D_STEP = 512


def swap(x, axis, distance):
    n = lax.axis_size(axis)
    return lax.ppermute(x, axis, [(i, i ^ distance) for i in range(n)])


def shift(x, axis, distance):
    n = lax.axis_size(axis)
    return lax.ppermute(x, axis, [(i, i + distance) for i in range(n - distance)])


def bits_down(n):
    return [1 << b for b in reversed(range(n.bit_length() - 1))]


def gather_swapped(x, axis):
    n = lax.axis_size(axis)
    x = x[None]
    for bit in bits_down(n):
        other = swap(x, axis, bit)
        size = x.shape[0]
        both = jnp.stack([x, other], 1)
        x = both.reshape((2 * size,) + x.shape[1:]) if size > 1 else both[0]
    return x


def attend(queries, keys, values, lengths, kv_here, split):
    tok = queries.shape[0]
    s = lax.axis_index("seq")
    e = lax.axis_index("exp")
    r = lax.axis_index("rep")
    n_exp = lax.axis_size("exp")
    per = max(1, kv_here // n_exp)
    rows = tok // split
    head = r * kv_here + (e // split) * per
    k = lax.dynamic_slice_in_dim(keys, head * HD, per * HD, 1)
    v = lax.dynamic_slice_in_dim(values, head * HD, per * HD, 1)
    kv = jnp.concatenate([k, v], axis=1)
    wide = [shift(kv, "seq", back) for back in range(REACH, 0, -1)] + [kv]
    wide = jnp.concatenate(wide, 0)
    span = (REACH + 1) * tok
    k_wide = wide[:, : per * HD].reshape(span, per, HD)
    v_wide = wide[:, per * HD :].reshape(span, per, HD)
    q = lax.dynamic_slice(
        queries, ((e % split) * rows, head * GROUP * HD), (rows, per * GROUP * HD)
    ).reshape(rows, per, GROUP, HD)
    ends = jnp.cumsum(lengths)
    q_pos = s * tok + (e % split) * rows + jnp.arange(rows, dtype=jnp.int32)
    k_pos = (s - REACH) * tok + jnp.arange(span, dtype=jnp.int32)
    q_seg = jnp.sum((q_pos[:, None] >= ends[None, :]).astype(jnp.int32), axis=1)
    k_seg = jnp.sum((k_pos[:, None] >= ends[None, :]).astype(jnp.int32), axis=1)
    allowed = (
        (q_seg[:, None] == k_seg[None, :])
        & (k_pos[None, :] <= q_pos[:, None])
        & (k_pos[None, :] >= 0)
    )
    scores = jnp.einsum(
        "tpjd,kpd->pjtk", q, k_wide, preferred_element_type=jnp.float32
    ) * HD ** (-0.5)
    scores = jnp.where(allowed[None, None], scores, -jnp.inf)
    top = jnp.max(scores, axis=-1, keepdims=True)
    weights = jnp.exp(scores - top)
    probs = (weights / jnp.sum(weights, axis=-1, keepdims=True)).astype(jnp.bfloat16)
    out = jnp.einsum("pjtk,kpd->tpjd", probs, v_wide, preferred_element_type=jnp.float32)
    return out.astype(jnp.bfloat16).reshape(rows, per * GROUP * HD)


def gather_tokens(own, tok, cols, split):
    n_seq = lax.axis_size("seq")
    n_exp = lax.axis_size("exp")
    e = lax.axis_index("exp")
    rows, width = own.shape
    pieces = [own] + [swap(own, "exp", d) for d in range(1, n_exp)]
    bunch = max(1, n_exp // 4)
    full = jnp.zeros((n_seq, tok, cols), jnp.bfloat16)
    for first in range(0, n_exp, bunch):
        held = jnp.stack(pieces[first : first + bunch])
        got = gather_swapped(held, "seq")
        for j in range(bunch):
            at = e ^ (first + j)
            full = lax.dynamic_update_slice(
                full, got[:, j], (0, (at % split) * rows, (at // split) * width)
            )
    return full.reshape(n_seq * tok, cols)


def expert_kernel(p_ref, wg_ref, wd_ref, out_ref, wbuf, kept, sent, got, hid, wsem, s1, r1, s2, r2):
    r = lax.axis_index("rep")
    partner = {"rep": 1 - r}
    owned, rows, cols = out_ref.shape
    hidden = wbuf.shape[1]
    pairs = owned // 2
    mine = [2 * p + r for p in range(pairs)]
    theirs = [2 * p + 1 - r for p in range(pairs)]
    blocks = [wg_ref.at[2 * e + g] for e in theirs + mine for g in range(2)]
    blocks += [wd_ref.at[e] for e in mine + theirs]

    def load(t):
        return pltpu.make_async_copy(blocks[t], wbuf.at[t % SLOTS], wsem.at[t % SLOTS])

    for t in range(SLOTS):
        load(t).start()
    barrier = pltpu.get_barrier_semaphore()
    pl.semaphore_signal(barrier, inc=1, device_id=partner, device_id_type=pl.DeviceIdType.MESH)
    pl.semaphore_wait(barrier, 1)

    def refill(t):
        if t + SLOTS < len(blocks):
            load(t + SLOTS).start()

    def gate_part(t, e, dst):
        load(t).wait()
        w = wbuf.at[t % SLOTS]

        def piece(start, size):
            acc = lax.dot_general(
                w[pl.ds(start, size), :],
                p_ref[e],
                (((1,), (1,)), ((), ())),
                preferred_element_type=jnp.float32,
            )
            dst[:, pl.ds(start, size)] = acc.T.astype(jnp.bfloat16)

        whole = hidden // F_STEP

        @pl.loop(0, whole)
        def _(k):
            piece(pl.multiple_of(k * F_STEP, F_STEP), F_STEP)

        if hidden % F_STEP:
            piece(whole * F_STEP, hidden % F_STEP)
        refill(t)

    def reduce_copy(p, g):
        return pltpu.make_async_remote_copy(
            src_ref=sent.at[p, g],
            dst_ref=got.at[p, g],
            send_sem=s1.at[p, g],
            recv_sem=r1.at[p, g],
            device_id=partner,
            device_id_type=pl.DeviceIdType.MESH,
        )

    def hidden_copy(p):
        return pltpu.make_async_remote_copy(
            src_ref=hid.at[0, p],
            dst_ref=hid.at[1, p],
            send_sem=s2.at[p],
            recv_sem=r2.at[p],
            device_id=partner,
            device_id_type=pl.DeviceIdType.MESH,
        )

    def down(t, e, side, p):
        load(t).wait()
        w = wbuf.at[t % SLOTS]

        @pl.loop(0, cols // D_STEP)
        def _(k):
            at = pl.ds(pl.multiple_of(k * D_STEP, D_STEP), D_STEP)
            acc = jnp.dot(hid[side, p], w[:, at], preferred_element_type=jnp.float32)
            out_ref[e, :, at] = acc.astype(jnp.bfloat16)

        refill(t)

    t = 0
    for p in range(pairs):
        for g in range(2):
            gate_part(t, theirs[p], sent.at[p, g])
            reduce_copy(p, g).start()
            t += 1
    for p in range(pairs):
        for g in range(2):
            gate_part(t, mine[p], kept.at[p, g])
            t += 1
    for p in range(pairs):
        for g in range(2):
            reduce_copy(p, g).wait_recv()

        @pl.loop(0, rows // 16)
        def _(k):
            at = pl.ds(pl.multiple_of(k * 16, 16), 16)
            gate = kept[p, 0, at, :].astype(jnp.float32) + got[p, 0, at, :].astype(jnp.float32)
            up = kept[p, 1, at, :].astype(jnp.float32) + got[p, 1, at, :].astype(jnp.float32)
            hid[0, p, at, :] = (gate / (1.0 + jnp.exp(-gate)) * up).astype(jnp.bfloat16)

        hidden_copy(p).start()
        down(t, mine[p], 0, p)
        t += 1
    for p in range(pairs):
        hidden_copy(p).wait_recv()
        down(t, theirs[p], 1, p)
        t += 1
    for p in range(pairs):
        for g in range(2):
            reduce_copy(p, g).wait_send()
        hidden_copy(p).wait_send()


def expert_rows(picked, gate_up, down_t):
    owned, rows, cols = picked.shape
    hidden = gate_up.shape[3]
    pairs = owned // 2
    wg = gate_up.transpose(0, 2, 3, 1).reshape(owned * 2, hidden, cols)
    wd = down_t.transpose(0, 2, 1)
    vmem = pl.BlockSpec(memory_space=pltpu.VMEM)
    hbm = pl.BlockSpec(memory_space=pl.ANY)
    half = (pairs, 2, rows, hidden)
    return pl.pallas_call(
        expert_kernel,
        out_shape=jax.ShapeDtypeStruct((owned, rows, cols), jnp.bfloat16),
        in_specs=[vmem, hbm, hbm],
        out_specs=vmem,
        scratch_shapes=[
            pltpu.VMEM((SLOTS, hidden, cols), jnp.bfloat16),
            pltpu.VMEM(half, jnp.bfloat16),
            pltpu.VMEM(half, jnp.bfloat16),
            pltpu.VMEM(half, jnp.bfloat16),
            pltpu.VMEM((2, pairs, rows, hidden), jnp.bfloat16),
            pltpu.SemaphoreType.DMA((SLOTS,)),
            pltpu.SemaphoreType.DMA((pairs, 2)),
            pltpu.SemaphoreType.DMA((pairs, 2)),
            pltpu.SemaphoreType.DMA((pairs,)),
            pltpu.SemaphoreType.DMA((pairs,)),
        ],
        compiler_params=pltpu.CompilerParams(
            collective_id=0, has_side_effects=True, vmem_limit_bytes=56 << 20
        ),
        cost_estimate=pl.CostEstimate(
            flops=6 * owned * rows * cols * hidden,
            bytes_accessed=6 * owned * cols * hidden,
            transcendentals=owned * rows * hidden,
        ),
    )(picked, wg, wd)


def per_device(queries, keys, values, lengths, expert_ids, gate_share, gate_up, down_t):
    n_seq = lax.axis_size("seq")
    n_exp = lax.axis_size("exp")
    n_rep = lax.axis_size("rep")
    tok = queries.shape[0]
    owned, cols = gate_up.shape[0], gate_up.shape[1]
    e = lax.axis_index("exp")
    r = lax.axis_index("rep")
    kv_here = cols // (GROUP * HD)
    split = max(1, n_exp // kv_here)

    table = jnp.concatenate([expert_ids.astype(jnp.float32).T, gate_share.T], 0)
    table = gather_swapped(table, "seq")
    ids = table[:, :TOPK].astype(jnp.int32)
    shares = table[:, TOPK:]
    mine = e * owned + jnp.arange(owned, dtype=jnp.int32)
    hit = ids[None] == mine[:, None, None, None]
    match = jnp.any(hit, axis=2)
    share = jnp.sum(jnp.where(hit, shares[None], 0.0), axis=2)
    count = match.astype(jnp.int32)
    rank = jnp.cumsum(count, axis=2) - count
    block = jnp.arange(n_seq, dtype=jnp.int32)[None, :, None]
    key = jnp.where(match, block * CAP + rank, -1)
    paired = n_rep == 2 and owned % 2 == 0 and cols % D_STEP == 0
    slots = n_seq * CAP
    rows = -(-slots // 16) * 16 if paired else slots
    part = slots // n_rep
    at = jnp.arange(rows, dtype=jnp.int32)
    if paired:
        slot = jnp.where(at < slots, at, -2)
    else:
        slot = (r ^ (at // part)) * part + at % part
    pick = (key.reshape(owned, 1, n_seq * tok) == slot[None, :, None]).astype(jnp.bfloat16)

    def turned(x):
        cut = x.reshape(owned, n_seq, n_exp, tok // n_exp)
        order = e ^ jnp.arange(n_exp, dtype=jnp.int32)
        return jnp.take(cut, order, axis=2).reshape(owned, n_seq * tok)

    key_out, share_out = turned(key), turned(share)
    spread = jnp.where(
        key_out.T[:, :, None] == slot[None, None, :], share_out.T[:, :, None], 0.0
    ).astype(jnp.bfloat16).reshape(n_seq * tok, owned * rows)

    own = attend(queries, keys, values, lengths, kv_here, split)
    tokens = gather_tokens(own, tok, cols, split)

    if paired:
        picked = jnp.dot(
            pick.reshape(owned * rows, n_seq * tok), tokens, preferred_element_type=jnp.float32
        ).astype(jnp.bfloat16)
        outs = expert_rows(picked.reshape(owned, rows, cols), gate_up, down_t)
        outs = outs.reshape(owned * rows, cols)
    else:
        outs = []
        for i in range(owned):
            picked = jnp.dot(pick[i], tokens, preferred_element_type=jnp.float32).astype(jnp.bfloat16)
            both = jnp.einsum("rd,dgf->grf", picked, gate_up[i], preferred_element_type=jnp.float32)
            both = both.astype(jnp.bfloat16)
            total = both[:, :part].astype(jnp.float32)
            for d in range(1, n_rep):
                got = swap(both[:, d * part : (d + 1) * part], "rep", d)
                total = total + got.astype(jnp.float32)
            hidden = (jax.nn.silu(total[0]) * total[1]).astype(jnp.bfloat16)
            hidden = jnp.concatenate([hidden] + [swap(hidden, "rep", d) for d in range(1, n_rep)], 0)
            down = jnp.einsum("rf,df->rd", hidden, down_t[i], preferred_element_type=jnp.float32)
            outs.append(down.astype(jnp.bfloat16))
        outs = jnp.concatenate(outs, 0)

    results = []
    wide = cols // TAIL_PIECES
    for c in range(TAIL_PIECES):
        term = jnp.dot(
            spread, outs[:, c * wide : (c + 1) * wide], preferred_element_type=jnp.float32
        ).astype(jnp.bfloat16).reshape(n_seq, tok, wide)
        for bit in reversed(bits_down(n_seq)):
            pairs = term.reshape(term.shape[0] // 2, 2, tok, wide)
            got = swap(pairs[:, 1], "seq", bit)
            term = (pairs[:, 0].astype(jnp.float32) + got.astype(jnp.float32)).astype(jnp.bfloat16)
        chunks = term.reshape(n_exp, tok // n_exp, wide)
        total = chunks[0].astype(jnp.float32)
        for d in range(1, n_exp):
            total = total + swap(chunks[d], "exp", d).astype(jnp.float32)
        results.append(total.astype(jnp.bfloat16))
    return jnp.concatenate(results, 1)


def solution(mesh):
    in_specs = (
        P("seq", None),
        P("seq", None),
        P("seq", None),
        P(),
        P("seq", None),
        P("seq", None),
        P("exp", "rep", None, "seq"),
        P("exp", "rep", "seq"),
    )
    out_specs = P(("seq", "exp"), "rep")
    return jax.shard_map(
        per_device, mesh=mesh, in_specs=in_specs, out_specs=out_specs, check_vma=False
    )
```

```python
import jax
import jax.numpy as jnp
from jax import lax
from jax.experimental import pallas as pl
from jax.experimental.pallas import tpu as pltpu
from jax.sharding import PartitionSpec as P

HEADS = 48
KV = 8
HD = 128
TOPK = 4
REACH = 2
CAP = 34
GROUP = HEADS // KV
TAIL_PIECES = 2
SLOTS = 4
F_STEP = 384
D_STEP = 512


def swap(x, axis, distance):
    n = lax.axis_size(axis)
    return lax.ppermute(x, axis, [(i, i ^ distance) for i in range(n)])


def shift(x, axis, distance):
    n = lax.axis_size(axis)
    return lax.ppermute(x, axis, [(i, i + distance) for i in range(n - distance)])


def bits_down(n):
    return [1 << b for b in reversed(range(n.bit_length() - 1))]


def gather_swapped(x, axis):
    n = lax.axis_size(axis)
    x = x[None]
    for bit in bits_down(n):
        other = swap(x, axis, bit)
        size = x.shape[0]
        both = jnp.stack([x, other], 1)
        x = both.reshape((2 * size,) + x.shape[1:]) if size > 1 else both[0]
    return x


def attend(queries, keys, values, lengths, kv_here, split):
    tok = queries.shape[0]
    s = lax.axis_index("seq")
    e = lax.axis_index("exp")
    r = lax.axis_index("rep")
    n_exp = lax.axis_size("exp")
    per = max(1, kv_here // n_exp)
    rows = tok // split
    head = r * kv_here + (e // split) * per
    k = lax.dynamic_slice_in_dim(keys, head * HD, per * HD, 1)
    v = lax.dynamic_slice_in_dim(values, head * HD, per * HD, 1)
    kv = jnp.concatenate([k, v], axis=1)
    wide = [shift(kv, "seq", back) for back in range(REACH, 0, -1)] + [kv]
    wide = jnp.concatenate(wide, 0)
    span = (REACH + 1) * tok
    k_wide = wide[:, : per * HD].reshape(span, per, HD)
    v_wide = wide[:, per * HD :].reshape(span, per, HD)
    q = lax.dynamic_slice(
        queries, ((e % split) * rows, head * GROUP * HD), (rows, per * GROUP * HD)
    ).reshape(rows, per, GROUP, HD)
    ends = jnp.cumsum(lengths)
    q_pos = s * tok + (e % split) * rows + jnp.arange(rows, dtype=jnp.int32)
    k_pos = (s - REACH) * tok + jnp.arange(span, dtype=jnp.int32)
    q_seg = jnp.sum((q_pos[:, None] >= ends[None, :]).astype(jnp.int32), axis=1)
    k_seg = jnp.sum((k_pos[:, None] >= ends[None, :]).astype(jnp.int32), axis=1)
    allowed = (
        (q_seg[:, None] == k_seg[None, :])
        & (k_pos[None, :] <= q_pos[:, None])
        & (k_pos[None, :] >= 0)
    )
    scores = jnp.einsum(
        "tpjd,kpd->pjtk", q, k_wide, preferred_element_type=jnp.float32
    ) * HD ** (-0.5)
    scores = jnp.where(allowed[None, None], scores, -jnp.inf)
    top = jnp.max(scores, axis=-1, keepdims=True)
    weights = jnp.exp(scores - top)
    probs = (weights / jnp.sum(weights, axis=-1, keepdims=True)).astype(jnp.bfloat16)
    out = jnp.einsum("pjtk,kpd->tpjd", probs, v_wide, preferred_element_type=jnp.float32)
    return out.astype(jnp.bfloat16).reshape(rows, per * GROUP * HD)


def gather_tokens(own, tok, cols, split):
    n_seq = lax.axis_size("seq")
    n_exp = lax.axis_size("exp")
    e = lax.axis_index("exp")
    rows, width = own.shape
    pieces = [own] + [swap(own, "exp", d) for d in range(1, n_exp)]
    bunch = max(1, n_exp // 4)
    full = jnp.zeros((n_seq, tok, cols), jnp.bfloat16)
    for first in range(0, n_exp, bunch):
        held = jnp.stack(pieces[first : first + bunch])
        got = gather_swapped(held, "seq")
        for j in range(bunch):
            at = e ^ (first + j)
            full = lax.dynamic_update_slice(
                full, got[:, j], (0, (at % split) * rows, (at // split) * width)
            )
    return full.reshape(n_seq * tok, cols)


def expert_kernel(p_ref, wg_ref, wd_ref, out_ref, wbuf, kept, sent, got, hid, wsem, s1, r1, s2, r2):
    r = lax.axis_index("rep")
    partner = {"rep": 1 - r}
    owned, rows, cols = out_ref.shape
    hidden = wbuf.shape[1]
    pairs = owned // 2
    mine = [2 * p + r for p in range(pairs)]
    theirs = [2 * p + 1 - r for p in range(pairs)]
    blocks = [wg_ref.at[2 * e + g] for e in theirs + mine for g in range(2)]
    blocks += [wd_ref.at[e] for e in mine + theirs]

    def load(t):
        return pltpu.make_async_copy(blocks[t], wbuf.at[t % SLOTS], wsem.at[t % SLOTS])

    for t in range(SLOTS):
        load(t).start()
    barrier = pltpu.get_barrier_semaphore()
    pl.semaphore_signal(barrier, inc=1, device_id=partner, device_id_type=pl.DeviceIdType.MESH)
    pl.semaphore_wait(barrier, 1)

    def refill(t):
        if t + SLOTS < len(blocks):
            load(t + SLOTS).start()

    def gate_part(t, e, dst):
        load(t).wait()
        w = wbuf.at[t % SLOTS]

        def piece(start, size):
            acc = lax.dot_general(
                w[pl.ds(start, size), :],
                p_ref[e],
                (((1,), (1,)), ((), ())),
                preferred_element_type=jnp.float32,
            )
            dst[:, pl.ds(start, size)] = acc.T.astype(jnp.bfloat16)

        whole = hidden // F_STEP

        @pl.loop(0, whole)
        def _(k):
            piece(pl.multiple_of(k * F_STEP, F_STEP), F_STEP)

        if hidden % F_STEP:
            piece(whole * F_STEP, hidden % F_STEP)
        refill(t)

    def reduce_copy(p, g):
        return pltpu.make_async_remote_copy(
            src_ref=sent.at[p, g],
            dst_ref=got.at[p, g],
            send_sem=s1.at[p, g],
            recv_sem=r1.at[p, g],
            device_id=partner,
            device_id_type=pl.DeviceIdType.MESH,
        )

    def hidden_copy(p):
        return pltpu.make_async_remote_copy(
            src_ref=hid.at[0, p],
            dst_ref=hid.at[1, p],
            send_sem=s2.at[p],
            recv_sem=r2.at[p],
            device_id=partner,
            device_id_type=pl.DeviceIdType.MESH,
        )

    def down(t, e, side, p):
        load(t).wait()
        w = wbuf.at[t % SLOTS]

        @pl.loop(0, cols // D_STEP)
        def _(k):
            at = pl.ds(pl.multiple_of(k * D_STEP, D_STEP), D_STEP)
            acc = jnp.dot(hid[side, p], w[:, at], preferred_element_type=jnp.float32)
            out_ref[e, :, at] = acc.astype(jnp.bfloat16)

        refill(t)

    t = 0
    for p in range(pairs):
        for g in range(2):
            gate_part(t, theirs[p], sent.at[p, g])
            reduce_copy(p, g).start()
            t += 1
    for p in range(pairs):
        for g in range(2):
            gate_part(t, mine[p], kept.at[p, g])
            t += 1
    for p in range(pairs):
        for g in range(2):
            reduce_copy(p, g).wait_recv()

        @pl.loop(0, rows // 16)
        def _(k):
            at = pl.ds(pl.multiple_of(k * 16, 16), 16)
            gate = kept[p, 0, at, :].astype(jnp.float32) + got[p, 0, at, :].astype(jnp.float32)
            up = kept[p, 1, at, :].astype(jnp.float32) + got[p, 1, at, :].astype(jnp.float32)
            hid[0, p, at, :] = (gate / (1.0 + jnp.exp(-gate)) * up).astype(jnp.bfloat16)

        hidden_copy(p).start()
        down(t, mine[p], 0, p)
        t += 1
    for p in range(pairs):
        hidden_copy(p).wait_recv()
        down(t, theirs[p], 1, p)
        t += 1
    for p in range(pairs):
        for g in range(2):
            reduce_copy(p, g).wait_send()
        hidden_copy(p).wait_send()


def expert_rows(picked, gate_up, down_t):
    owned, rows, cols = picked.shape
    hidden = gate_up.shape[3]
    pairs = owned // 2
    wg = gate_up.transpose(0, 2, 3, 1).reshape(owned * 2, hidden, cols)
    wd = down_t.transpose(0, 2, 1)
    vmem = pl.BlockSpec(memory_space=pltpu.VMEM)
    hbm = pl.BlockSpec(memory_space=pl.ANY)
    half = (pairs, 2, rows, hidden)
    return pl.pallas_call(
        expert_kernel,
        out_shape=jax.ShapeDtypeStruct((owned, rows, cols), jnp.bfloat16),
        in_specs=[vmem, hbm, hbm],
        out_specs=vmem,
        scratch_shapes=[
            pltpu.VMEM((SLOTS, hidden, cols), jnp.bfloat16),
            pltpu.VMEM(half, jnp.bfloat16),
            pltpu.VMEM(half, jnp.bfloat16),
            pltpu.VMEM(half, jnp.bfloat16),
            pltpu.VMEM((2, pairs, rows, hidden), jnp.bfloat16),
            pltpu.SemaphoreType.DMA((SLOTS,)),
            pltpu.SemaphoreType.DMA((pairs, 2)),
            pltpu.SemaphoreType.DMA((pairs, 2)),
            pltpu.SemaphoreType.DMA((pairs,)),
            pltpu.SemaphoreType.DMA((pairs,)),
        ],
        compiler_params=pltpu.CompilerParams(
            collective_id=0, has_side_effects=True, vmem_limit_bytes=56 << 20
        ),
        cost_estimate=pl.CostEstimate(
            flops=6 * owned * rows * cols * hidden,
            bytes_accessed=6 * owned * cols * hidden,
            transcendentals=owned * rows * hidden,
        ),
    )(picked, wg, wd)


def greet(partners):
    barrier = pltpu.get_barrier_semaphore()
    for partner in partners:
        pl.semaphore_signal(barrier, inc=1, device_id=partner, device_id_type=pl.DeviceIdType.MESH)
    pl.semaphore_wait(barrier, len(partners))


def plane():
    s = lax.axis_index("seq")
    e = lax.axis_index("exp")
    n = lax.axis_size("exp")
    near = {"seq": s + 1 - 2 * (s % 2)}
    far = {"seq": (s + 2) % 4}
    return near, far, [{"exp": (e + d) % n} for d in range(n)]


def remote(src, dst, send, recv, device):
    return pltpu.make_async_remote_copy(
        src_ref=src,
        dst_ref=dst,
        send_sem=send,
        recv_sem=recv,
        device_id=device,
        device_id_type=pl.DeviceIdType.MESH,
    )


def gather_kernel(own, out, zs, zr, ys, yr, cs, cr):
    e = lax.axis_index("exp")
    n = lax.axis_size("exp")
    width = own.shape[1]
    near, far, line = plane()

    def columns(d):
        return pl.ds(pl.multiple_of(((e + n - d) % n) * width, 128), width)

    def along_exp(d):
        return remote(own, out.at[0, :, columns(0)], zs.at[d], zr.at[d], line[d])

    def along_y(d):
        src = own if d == 0 else out.at[0, :, columns(d)]
        return remote(src, out.at[2, :, columns(d)], ys.at[d], yr.at[d], far)

    def along_core(d, q):
        src = own if d == 0 and q == 0 else out.at[2 * q, :, columns(d)]
        return remote(src, out.at[2 * q + 1, :, columns(d)], cs.at[d, q], cr.at[d, q], near)

    greet([near, far] + line[1:])
    for d in range(1, n):
        along_exp(d).start()
    along_y(0).start()
    along_core(0, 0).start()
    out[0, :, columns(0)] = own[...]
    for d in range(1, n):
        along_exp(d).wait_recv()
        along_y(d).start()
        along_core(d, 0).start()
        along_y(d - 1).wait_recv()
        along_core(d - 1, 1).start()
    along_y(n - 1).wait_recv()
    along_core(n - 1, 1).start()
    for d in range(n):
        for q in range(2):
            along_core(d, q).wait()
        along_y(d).wait_send()
        if d:
            along_exp(d).wait_send()


def gather_plane(own, tok, cols):
    n = lax.axis_size("exp")
    vmem = pl.BlockSpec(memory_space=pltpu.VMEM)
    sems = [pltpu.SemaphoreType.DMA((n,))] * 4 + [pltpu.SemaphoreType.DMA((n, 2))] * 2
    return pl.pallas_call(
        gather_kernel,
        out_shape=jax.ShapeDtypeStruct((4, tok, cols), jnp.bfloat16),
        in_specs=[vmem],
        out_specs=vmem,
        scratch_shapes=sems,
        compiler_params=pltpu.CompilerParams(
            collective_id=1, has_side_effects=True, vmem_limit_bytes=16 << 20
        ),
    )(own).reshape(4 * tok, cols)


def combine_kernel(spread, rows, out, term, cgot, half, ygot, quarter, zgot, cs, cr, ys, yr, zs, zr):
    n = lax.axis_size("exp")
    pieces, _, _, tok, width = term.shape
    mine = tok // n
    near, far, line = plane()

    def along_core(c):
        return remote(term.at[c, 1], cgot.at[c], cs.at[c], cr.at[c], near)

    def along_y(c):
        return remote(half.at[c, 1], ygot.at[c], ys.at[c], yr.at[c], far)

    def along_exp(c, d):
        src = quarter.at[c, pl.ds(d * mine, mine)]
        return remote(src, zgot.at[c, d], zs.at[c, d], zr.at[c, d], line[d])

    def wide(x):
        return x.astype(jnp.float32)

    def first(c):
        for q in (1, 3, 0, 2):
            acc = jnp.dot(
                spread[q * tok : (q + 1) * tok, :],
                rows[:, c * width : (c + 1) * width],
                preferred_element_type=jnp.float32,
            )
            term[c, q % 2, q // 2] = acc.astype(jnp.bfloat16)
        along_core(c).start()

    def second(c):
        along_core(c).wait_recv()
        half[c, 1] = (wide(term[c, 0, 1]) + wide(cgot[c, 1])).astype(jnp.bfloat16)
        along_y(c).start()
        half[c, 0] = (wide(term[c, 0, 0]) + wide(cgot[c, 0])).astype(jnp.bfloat16)

    def third(c):
        along_y(c).wait_recv()
        quarter[c] = (wide(half[c, 0]) + wide(ygot[c])).astype(jnp.bfloat16)
        for d in range(1, n):
            along_exp(c, d).start()

    greet([near, far] + line[1:])
    for c in range(pieces + 2):
        if c < pieces:
            first(c)
        if 1 <= c <= pieces:
            second(c - 1)
        if c >= 2:
            third(c - 2)
    for c in range(pieces):
        total = wide(quarter[c, :mine])
        for d in range(1, n):
            along_exp(c, d).wait_recv()
            total = total + wide(zgot[c, d])
        out[:, c * width : (c + 1) * width] = total.astype(jnp.bfloat16)
    for c in range(pieces):
        along_core(c).wait_send()
        along_y(c).wait_send()
        for d in range(1, n):
            along_exp(c, d).wait_send()


def combine_plane(spread, rows, tok):
    n = lax.axis_size("exp")
    cols = rows.shape[1]
    c, w = 4, cols // 4
    vmem = pl.BlockSpec(memory_space=pltpu.VMEM)
    shapes = [(c, 2, 2, tok, w), (c, 2, tok, w), (c, 2, tok, w), (c, tok, w), (c, tok, w)]
    shapes.append((c, n, tok // n, w))
    sems = [pltpu.SemaphoreType.DMA((c,))] * 4 + [pltpu.SemaphoreType.DMA((c, n))] * 2
    return pl.pallas_call(
        combine_kernel,
        out_shape=jax.ShapeDtypeStruct((tok // n, cols), jnp.bfloat16),
        in_specs=[vmem, vmem],
        out_specs=vmem,
        scratch_shapes=[pltpu.VMEM(shape, jnp.bfloat16) for shape in shapes] + sems,
        compiler_params=pltpu.CompilerParams(
            collective_id=2, has_side_effects=True, vmem_limit_bytes=32 << 20
        ),
    )(spread, rows)


def per_device(queries, keys, values, lengths, expert_ids, gate_share, gate_up, down_t):
    n_seq = lax.axis_size("seq")
    n_exp = lax.axis_size("exp")
    n_rep = lax.axis_size("rep")
    tok = queries.shape[0]
    owned, cols = gate_up.shape[0], gate_up.shape[1]
    e = lax.axis_index("exp")
    r = lax.axis_index("rep")
    kv_here = cols // (GROUP * HD)
    split = max(1, n_exp // kv_here)

    table = jnp.concatenate([expert_ids.astype(jnp.float32).T, gate_share.T], 0)
    table = gather_swapped(table, "seq")
    ids = table[:, :TOPK].astype(jnp.int32)
    shares = table[:, TOPK:]
    mine = e * owned + jnp.arange(owned, dtype=jnp.int32)
    hit = ids[None] == mine[:, None, None, None]
    match = jnp.any(hit, axis=2)
    share = jnp.sum(jnp.where(hit, shares[None], 0.0), axis=2)
    count = match.astype(jnp.int32)
    rank = jnp.cumsum(count, axis=2) - count
    block = jnp.arange(n_seq, dtype=jnp.int32)[None, :, None]
    key = jnp.where(match, block * CAP + rank, -1)
    paired = n_rep == 2 and owned % 2 == 0 and cols % D_STEP == 0
    compact = paired and n_seq == 4 and split == 1 and kv_here == n_exp and cols % 512 == 0
    slots = n_seq * CAP
    rows = -(-slots // 16) * 16 if paired else slots
    part = slots // n_rep
    at = jnp.arange(rows, dtype=jnp.int32)
    if paired:
        slot = jnp.where(at < slots, at, -2)
    else:
        slot = (r ^ (at // part)) * part + at % part
    pick = (key.reshape(owned, 1, n_seq * tok) == slot[None, :, None]).astype(jnp.bfloat16)

    def turned(x):
        cut = x.reshape(owned, n_seq, n_exp, tok // n_exp)
        order = jnp.arange(n_exp, dtype=jnp.int32)
        order = (e + order) % n_exp if compact else e ^ order
        return jnp.take(cut, order, axis=2).reshape(owned, n_seq * tok)

    key_out, share_out = turned(key), turned(share)
    spread = jnp.where(
        key_out.T[:, :, None] == slot[None, None, :], share_out.T[:, :, None], 0.0
    ).astype(jnp.bfloat16).reshape(n_seq * tok, owned * rows)

    own = attend(queries, keys, values, lengths, kv_here, split)
    if compact:
        tokens = gather_plane(own, tok, cols)
    else:
        tokens = gather_tokens(own, tok, cols, split)

    if paired:
        picked = jnp.dot(
            pick.reshape(owned * rows, n_seq * tok), tokens, preferred_element_type=jnp.float32
        ).astype(jnp.bfloat16)
        outs = expert_rows(picked.reshape(owned, rows, cols), gate_up, down_t)
        outs = outs.reshape(owned * rows, cols)
    else:
        outs = []
        for i in range(owned):
            picked = jnp.dot(pick[i], tokens, preferred_element_type=jnp.float32).astype(jnp.bfloat16)
            both = jnp.einsum("rd,dgf->grf", picked, gate_up[i], preferred_element_type=jnp.float32)
            both = both.astype(jnp.bfloat16)
            total = both[:, :part].astype(jnp.float32)
            for d in range(1, n_rep):
                got = swap(both[:, d * part : (d + 1) * part], "rep", d)
                total = total + got.astype(jnp.float32)
            hidden = (jax.nn.silu(total[0]) * total[1]).astype(jnp.bfloat16)
            hidden = jnp.concatenate([hidden] + [swap(hidden, "rep", d) for d in range(1, n_rep)], 0)
            down = jnp.einsum("rf,df->rd", hidden, down_t[i], preferred_element_type=jnp.float32)
            outs.append(down.astype(jnp.bfloat16))
        outs = jnp.concatenate(outs, 0)

    if compact:
        return combine_plane(spread, outs, tok)

    results = []
    wide = cols // TAIL_PIECES
    for c in range(TAIL_PIECES):
        term = jnp.dot(
            spread, outs[:, c * wide : (c + 1) * wide], preferred_element_type=jnp.float32
        ).astype(jnp.bfloat16).reshape(n_seq, tok, wide)
        for bit in reversed(bits_down(n_seq)):
            pairs = term.reshape(term.shape[0] // 2, 2, tok, wide)
            got = swap(pairs[:, 1], "seq", bit)
            term = (pairs[:, 0].astype(jnp.float32) + got.astype(jnp.float32)).astype(jnp.bfloat16)
        chunks = term.reshape(n_exp, tok // n_exp, wide)
        total = chunks[0].astype(jnp.float32)
        for d in range(1, n_exp):
            total = total + swap(chunks[d], "exp", d).astype(jnp.float32)
        results.append(total.astype(jnp.bfloat16))
    return jnp.concatenate(results, 1)


def solution(mesh):
    in_specs = (
        P("seq", None),
        P("seq", None),
        P("seq", None),
        P(),
        P("seq", None),
        P("seq", None),
        P("exp", "rep", None, "seq"),
        P("exp", "rep", "seq"),
    )
    out_specs = P(("seq", "exp"), "rep")
    return jax.shard_map(
        per_device, mesh=mesh, in_specs=in_specs, out_specs=out_specs, check_vma=False
    )
```

```python
import jax
import jax.numpy as jnp
from jax import lax
from jax.experimental import pallas as pl
from jax.experimental.pallas import tpu as pltpu
from jax.sharding import PartitionSpec as P

HEADS = 48
KV = 8
HD = 128
TOPK = 4
REACH = 2
CAP = 34
GROUP = HEADS // KV
TAIL_PIECES = 2
SLOTS = 4
F_STEP = 384
D_STEP = 512


def swap(x, axis, distance):
    n = lax.axis_size(axis)
    return lax.ppermute(x, axis, [(i, i ^ distance) for i in range(n)])


def shift(x, axis, distance):
    n = lax.axis_size(axis)
    return lax.ppermute(x, axis, [(i, i + distance) for i in range(n - distance)])


def bits_down(n):
    return [1 << b for b in reversed(range(n.bit_length() - 1))]


def gather_swapped(x, axis):
    n = lax.axis_size(axis)
    x = x[None]
    for bit in bits_down(n):
        other = swap(x, axis, bit)
        size = x.shape[0]
        both = jnp.stack([x, other], 1)
        x = both.reshape((2 * size,) + x.shape[1:]) if size > 1 else both[0]
    return x


def attend(queries, keys, values, lengths, kv_here, split):
    tok = queries.shape[0]
    s = lax.axis_index("seq")
    e = lax.axis_index("exp")
    r = lax.axis_index("rep")
    n_exp = lax.axis_size("exp")
    per = max(1, kv_here // n_exp)
    rows = tok // split
    head = r * kv_here + (e // split) * per
    k = lax.dynamic_slice_in_dim(keys, head * HD, per * HD, 1)
    v = lax.dynamic_slice_in_dim(values, head * HD, per * HD, 1)
    kv = jnp.concatenate([k, v], axis=1)
    wide = [shift(kv, "seq", back) for back in range(REACH, 0, -1)] + [kv]
    wide = jnp.concatenate(wide, 0)
    span = (REACH + 1) * tok
    k_wide = wide[:, : per * HD].reshape(span, per, HD)
    v_wide = wide[:, per * HD :].reshape(span, per, HD)
    q = lax.dynamic_slice(
        queries, ((e % split) * rows, head * GROUP * HD), (rows, per * GROUP * HD)
    ).reshape(rows, per, GROUP, HD)
    ends = jnp.cumsum(lengths)
    q_pos = s * tok + (e % split) * rows + jnp.arange(rows, dtype=jnp.int32)
    k_pos = (s - REACH) * tok + jnp.arange(span, dtype=jnp.int32)
    q_seg = jnp.sum((q_pos[:, None] >= ends[None, :]).astype(jnp.int32), axis=1)
    k_seg = jnp.sum((k_pos[:, None] >= ends[None, :]).astype(jnp.int32), axis=1)
    allowed = (
        (q_seg[:, None] == k_seg[None, :])
        & (k_pos[None, :] <= q_pos[:, None])
        & (k_pos[None, :] >= 0)
    )
    scores = jnp.einsum(
        "tpjd,kpd->pjtk", q, k_wide, preferred_element_type=jnp.float32
    ) * HD ** (-0.5)
    scores = jnp.where(allowed[None, None], scores, -jnp.inf)
    top = jnp.max(scores, axis=-1, keepdims=True)
    weights = jnp.exp(scores - top)
    probs = (weights / jnp.sum(weights, axis=-1, keepdims=True)).astype(jnp.bfloat16)
    out = jnp.einsum("pjtk,kpd->tpjd", probs, v_wide, preferred_element_type=jnp.float32)
    return out.astype(jnp.bfloat16).reshape(rows, per * GROUP * HD)


def gather_tokens(own, tok, cols, split):
    n_seq = lax.axis_size("seq")
    n_exp = lax.axis_size("exp")
    e = lax.axis_index("exp")
    rows, width = own.shape
    pieces = [own] + [swap(own, "exp", d) for d in range(1, n_exp)]
    bunch = max(1, n_exp // 4)
    full = jnp.zeros((n_seq, tok, cols), jnp.bfloat16)
    for first in range(0, n_exp, bunch):
        held = jnp.stack(pieces[first : first + bunch])
        got = gather_swapped(held, "seq")
        for j in range(bunch):
            at = e ^ (first + j)
            full = lax.dynamic_update_slice(
                full, got[:, j], (0, (at % split) * rows, (at // split) * width)
            )
    return full.reshape(n_seq * tok, cols)


def expert_kernel(pick_ref, tok_ref, wg_ref, wd_ref, out_ref, p_ref, wbuf, kept, sent, got, hid, wsem, s1, r1, s2, r2):
    r = lax.axis_index("rep")
    partner = {"rep": 1 - r}
    owned, rows, cols = out_ref.shape
    hidden = wbuf.shape[1]
    pairs = owned // 2
    mine = [2 * p + r for p in range(pairs)]
    theirs = [2 * p + 1 - r for p in range(pairs)]
    blocks = [wg_ref.at[2 * e + g] for e in theirs + mine for g in range(2)]
    blocks += [wd_ref.at[e] for e in mine + theirs]

    def load(t):
        return pltpu.make_async_copy(blocks[t], wbuf.at[t % SLOTS], wsem.at[t % SLOTS])

    for t in range(SLOTS):
        load(t).start()
    barrier = pltpu.get_barrier_semaphore()
    pl.semaphore_signal(barrier, inc=1, device_id=partner, device_id_type=pl.DeviceIdType.MESH)
    pl.semaphore_wait(barrier, 1)

    def refill(t):
        if t + SLOTS < len(blocks):
            load(t + SLOTS).start()

    def pick_rows(e):
        @pl.loop(0, cols // D_STEP)
        def _(k):
            at = pl.ds(pl.multiple_of(k * D_STEP, D_STEP), D_STEP)
            acc = jnp.dot(pick_ref[e], tok_ref[:, at], preferred_element_type=jnp.float32)
            p_ref[e, :, at] = acc.astype(jnp.bfloat16)

    def gate_part(t, e, dst):
        load(t).wait()
        w = wbuf.at[t % SLOTS]

        def piece(start, size):
            acc = lax.dot_general(
                w[pl.ds(start, size), :],
                p_ref[e],
                (((1,), (1,)), ((), ())),
                preferred_element_type=jnp.float32,
            )
            dst[:, pl.ds(start, size)] = acc.T.astype(jnp.bfloat16)

        whole = hidden // F_STEP

        @pl.loop(0, whole)
        def _(k):
            piece(pl.multiple_of(k * F_STEP, F_STEP), F_STEP)

        if hidden % F_STEP:
            piece(whole * F_STEP, hidden % F_STEP)
        refill(t)

    def reduce_copy(p, g):
        return pltpu.make_async_remote_copy(
            src_ref=sent.at[p, g],
            dst_ref=got.at[p, g],
            send_sem=s1.at[p, g],
            recv_sem=r1.at[p, g],
            device_id=partner,
            device_id_type=pl.DeviceIdType.MESH,
        )

    def hidden_copy(p):
        return pltpu.make_async_remote_copy(
            src_ref=hid.at[0, p],
            dst_ref=hid.at[1, p],
            send_sem=s2.at[p],
            recv_sem=r2.at[p],
            device_id=partner,
            device_id_type=pl.DeviceIdType.MESH,
        )

    def down(t, e, side, p):
        load(t).wait()
        w = wbuf.at[t % SLOTS]

        @pl.loop(0, cols // D_STEP)
        def _(k):
            at = pl.ds(pl.multiple_of(k * D_STEP, D_STEP), D_STEP)
            acc = jnp.dot(hid[side, p], w[:, at], preferred_element_type=jnp.float32)
            out_ref[e, :, at] = acc.astype(jnp.bfloat16)

        refill(t)

    t = 0
    for p in range(pairs):
        pick_rows(theirs[p])
        for g in range(2):
            gate_part(t, theirs[p], sent.at[p, g])
            reduce_copy(p, g).start()
            t += 1
    for p in range(pairs):
        pick_rows(mine[p])
        for g in range(2):
            gate_part(t, mine[p], kept.at[p, g])
            t += 1
    for p in range(pairs):
        for g in range(2):
            reduce_copy(p, g).wait_recv()

        @pl.loop(0, rows // 16)
        def _(k):
            at = pl.ds(pl.multiple_of(k * 16, 16), 16)
            gate = kept[p, 0, at, :].astype(jnp.float32) + got[p, 0, at, :].astype(jnp.float32)
            up = kept[p, 1, at, :].astype(jnp.float32) + got[p, 1, at, :].astype(jnp.float32)
            hid[0, p, at, :] = (gate / (1.0 + jnp.exp(-gate)) * up).astype(jnp.bfloat16)

        hidden_copy(p).start()
        down(t, mine[p], 0, p)
        t += 1
    for p in range(pairs):
        hidden_copy(p).wait_recv()
        down(t, theirs[p], 1, p)
        t += 1
    for p in range(pairs):
        for g in range(2):
            reduce_copy(p, g).wait_send()
        hidden_copy(p).wait_send()


def expert_rows(pick, tokens, gate_up, down_t):
    owned, rows, _ = pick.shape
    cols = tokens.shape[1]
    hidden = gate_up.shape[3]
    pairs = owned // 2
    wg = gate_up.transpose(0, 2, 3, 1).reshape(owned * 2, hidden, cols)
    wd = down_t.transpose(0, 2, 1)
    vmem = pl.BlockSpec(memory_space=pltpu.VMEM)
    hbm = pl.BlockSpec(memory_space=pl.ANY)
    half = (pairs, 2, rows, hidden)
    return pl.pallas_call(
        expert_kernel,
        out_shape=jax.ShapeDtypeStruct((owned, rows, cols), jnp.bfloat16),
        in_specs=[vmem, vmem, hbm, hbm],
        out_specs=vmem,
        scratch_shapes=[
            pltpu.VMEM((owned, rows, cols), jnp.bfloat16),
            pltpu.VMEM((SLOTS, hidden, cols), jnp.bfloat16),
            pltpu.VMEM(half, jnp.bfloat16),
            pltpu.VMEM(half, jnp.bfloat16),
            pltpu.VMEM(half, jnp.bfloat16),
            pltpu.VMEM((2, pairs, rows, hidden), jnp.bfloat16),
            pltpu.SemaphoreType.DMA((SLOTS,)),
            pltpu.SemaphoreType.DMA((pairs, 2)),
            pltpu.SemaphoreType.DMA((pairs, 2)),
            pltpu.SemaphoreType.DMA((pairs,)),
            pltpu.SemaphoreType.DMA((pairs,)),
        ],
        compiler_params=pltpu.CompilerParams(
            collective_id=0, has_side_effects=True, vmem_limit_bytes=56 << 20
        ),
        cost_estimate=pl.CostEstimate(
            flops=6 * owned * rows * cols * hidden,
            bytes_accessed=6 * owned * cols * hidden,
            transcendentals=owned * rows * hidden,
        ),
    )(pick, tokens, wg, wd)


def greet(partners):
    barrier = pltpu.get_barrier_semaphore()
    for partner in partners:
        pl.semaphore_signal(barrier, inc=1, device_id=partner, device_id_type=pl.DeviceIdType.MESH)
    pl.semaphore_wait(barrier, len(partners))


def plane():
    s = lax.axis_index("seq")
    e = lax.axis_index("exp")
    n = lax.axis_size("exp")
    near = {"seq": s + 1 - 2 * (s % 2)}
    far = {"seq": (s + 2) % 4}
    return near, far, [{"exp": (e + d) % n} for d in range(n)]


def remote(src, dst, send, recv, device):
    return pltpu.make_async_remote_copy(
        src_ref=src,
        dst_ref=dst,
        send_sem=send,
        recv_sem=recv,
        device_id=device,
        device_id_type=pl.DeviceIdType.MESH,
    )


def gather_kernel(own, out, zs, zr, ys, yr, cs, cr):
    e = lax.axis_index("exp")
    n = lax.axis_size("exp")
    width = own.shape[1]
    near, far, line = plane()

    def columns(d):
        return pl.ds(pl.multiple_of(((e + n - d) % n) * width, 128), width)

    def along_exp(d):
        return remote(own, out.at[0, :, columns(0)], zs.at[d], zr.at[d], line[d])

    def along_y(d):
        src = own if d == 0 else out.at[0, :, columns(d)]
        return remote(src, out.at[2, :, columns(d)], ys.at[d], yr.at[d], far)

    def along_core(d, q):
        src = own if d == 0 and q == 0 else out.at[2 * q, :, columns(d)]
        return remote(src, out.at[2 * q + 1, :, columns(d)], cs.at[d, q], cr.at[d, q], near)

    greet([near, far] + line[1:])
    for d in range(1, n):
        along_exp(d).start()
    along_y(0).start()
    along_core(0, 0).start()
    out[0, :, columns(0)] = own[...]
    for d in range(1, n):
        along_exp(d).wait_recv()
        along_y(d).start()
        along_core(d, 0).start()
        along_y(d - 1).wait_recv()
        along_core(d - 1, 1).start()
    along_y(n - 1).wait_recv()
    along_core(n - 1, 1).start()
    for d in range(n):
        for q in range(2):
            along_core(d, q).wait()
        along_y(d).wait_send()
        if d:
            along_exp(d).wait_send()


def gather_plane(own, tok, cols):
    n = lax.axis_size("exp")
    vmem = pl.BlockSpec(memory_space=pltpu.VMEM)
    sems = [pltpu.SemaphoreType.DMA((n,))] * 4 + [pltpu.SemaphoreType.DMA((n, 2))] * 2
    return pl.pallas_call(
        gather_kernel,
        out_shape=jax.ShapeDtypeStruct((4, tok, cols), jnp.bfloat16),
        in_specs=[vmem],
        out_specs=vmem,
        scratch_shapes=sems,
        compiler_params=pltpu.CompilerParams(
            collective_id=1, has_side_effects=True, vmem_limit_bytes=16 << 20
        ),
    )(own).reshape(4 * tok, cols)


def combine_kernel(spread, rows, out, term, cgot, half, ygot, quarter, zgot, cs, cr, ys, yr, zs, zr):
    n = lax.axis_size("exp")
    pieces, _, _, tok, width = term.shape
    mine = tok // n
    near, far, line = plane()

    def along_core(c):
        return remote(term.at[c, 1], cgot.at[c], cs.at[c], cr.at[c], near)

    def along_y(c):
        return remote(half.at[c, 1], ygot.at[c], ys.at[c], yr.at[c], far)

    def along_exp(c, d):
        src = quarter.at[c, pl.ds(d * mine, mine)]
        return remote(src, zgot.at[c, d], zs.at[c, d], zr.at[c, d], line[d])

    def wide(x):
        return x.astype(jnp.float32)

    def first(c):
        for q in (1, 3, 0, 2):
            acc = jnp.dot(
                spread[q * tok : (q + 1) * tok, :],
                rows[:, c * width : (c + 1) * width],
                preferred_element_type=jnp.float32,
            )
            term[c, q % 2, q // 2] = acc.astype(jnp.bfloat16)
        along_core(c).start()

    def second(c):
        along_core(c).wait_recv()
        half[c, 1] = (wide(term[c, 0, 1]) + wide(cgot[c, 1])).astype(jnp.bfloat16)
        along_y(c).start()
        half[c, 0] = (wide(term[c, 0, 0]) + wide(cgot[c, 0])).astype(jnp.bfloat16)

    def third(c):
        along_y(c).wait_recv()
        quarter[c] = (wide(half[c, 0]) + wide(ygot[c])).astype(jnp.bfloat16)
        for d in range(1, n):
            along_exp(c, d).start()

    greet([near, far] + line[1:])
    for c in range(pieces + 2):
        if c < pieces:
            first(c)
        if 1 <= c <= pieces:
            second(c - 1)
        if c >= 2:
            third(c - 2)
    for c in range(pieces):
        total = wide(quarter[c, :mine])
        for d in range(1, n):
            along_exp(c, d).wait_recv()
            total = total + wide(zgot[c, d])
        out[:, c * width : (c + 1) * width] = total.astype(jnp.bfloat16)
    for c in range(pieces):
        along_core(c).wait_send()
        along_y(c).wait_send()
        for d in range(1, n):
            along_exp(c, d).wait_send()


def combine_plane(spread, rows, tok):
    n = lax.axis_size("exp")
    cols = rows.shape[1]
    c, w = 4, cols // 4
    vmem = pl.BlockSpec(memory_space=pltpu.VMEM)
    shapes = [(c, 2, 2, tok, w), (c, 2, tok, w), (c, 2, tok, w), (c, tok, w), (c, tok, w)]
    shapes.append((c, n, tok // n, w))
    sems = [pltpu.SemaphoreType.DMA((c,))] * 4 + [pltpu.SemaphoreType.DMA((c, n))] * 2
    return pl.pallas_call(
        combine_kernel,
        out_shape=jax.ShapeDtypeStruct((tok // n, cols), jnp.bfloat16),
        in_specs=[vmem, vmem],
        out_specs=vmem,
        scratch_shapes=[pltpu.VMEM(shape, jnp.bfloat16) for shape in shapes] + sems,
        compiler_params=pltpu.CompilerParams(
            collective_id=2, has_side_effects=True, vmem_limit_bytes=32 << 20
        ),
    )(spread, rows)


def per_device(queries, keys, values, lengths, expert_ids, gate_share, gate_up, down_t):
    n_seq = lax.axis_size("seq")
    n_exp = lax.axis_size("exp")
    n_rep = lax.axis_size("rep")
    tok = queries.shape[0]
    owned, cols = gate_up.shape[0], gate_up.shape[1]
    e = lax.axis_index("exp")
    r = lax.axis_index("rep")
    kv_here = cols // (GROUP * HD)
    split = max(1, n_exp // kv_here)

    table = jnp.concatenate([expert_ids.astype(jnp.float32).T, gate_share.T], 0)
    table = gather_swapped(table, "seq")
    ids = table[:, :TOPK].astype(jnp.int32)
    shares = table[:, TOPK:]
    mine = e * owned + jnp.arange(owned, dtype=jnp.int32)
    hit = ids[None] == mine[:, None, None, None]
    match = jnp.any(hit, axis=2)
    share = jnp.sum(jnp.where(hit, shares[None], 0.0), axis=2)
    count = match.astype(jnp.int32)
    rank = jnp.cumsum(count, axis=2) - count
    block = jnp.arange(n_seq, dtype=jnp.int32)[None, :, None]
    key = jnp.where(match, block * CAP + rank, -1)
    paired = n_rep == 2 and owned % 2 == 0 and cols % D_STEP == 0
    compact = paired and n_seq == 4 and split == 1 and kv_here == n_exp and cols % 512 == 0
    slots = n_seq * CAP
    rows = -(-slots // 16) * 16 if paired else slots
    part = slots // n_rep
    at = jnp.arange(rows, dtype=jnp.int32)
    if paired:
        slot = jnp.where(at < slots, at, -2)
    else:
        slot = (r ^ (at // part)) * part + at % part
    pick = (key.reshape(owned, 1, n_seq * tok) == slot[None, :, None]).astype(jnp.bfloat16)

    def turned(x):
        cut = x.reshape(owned, n_seq, n_exp, tok // n_exp)
        order = jnp.arange(n_exp, dtype=jnp.int32)
        order = (e + order) % n_exp if compact else e ^ order
        return jnp.take(cut, order, axis=2).reshape(owned, n_seq * tok)

    key_out, share_out = turned(key), turned(share)
    spread = jnp.where(
        key_out.T[:, :, None] == slot[None, None, :], share_out.T[:, :, None], 0.0
    ).astype(jnp.bfloat16).reshape(n_seq * tok, owned * rows)

    own = attend(queries, keys, values, lengths, kv_here, split)
    if compact:
        tokens = gather_plane(own, tok, cols)
    else:
        tokens = gather_tokens(own, tok, cols, split)

    if paired:
        outs = expert_rows(pick, tokens, gate_up, down_t)
        outs = outs.reshape(owned * rows, cols)
    else:
        outs = []
        for i in range(owned):
            picked = jnp.dot(pick[i], tokens, preferred_element_type=jnp.float32).astype(jnp.bfloat16)
            both = jnp.einsum("rd,dgf->grf", picked, gate_up[i], preferred_element_type=jnp.float32)
            both = both.astype(jnp.bfloat16)
            total = both[:, :part].astype(jnp.float32)
            for d in range(1, n_rep):
                got = swap(both[:, d * part : (d + 1) * part], "rep", d)
                total = total + got.astype(jnp.float32)
            hidden = (jax.nn.silu(total[0]) * total[1]).astype(jnp.bfloat16)
            hidden = jnp.concatenate([hidden] + [swap(hidden, "rep", d) for d in range(1, n_rep)], 0)
            down = jnp.einsum("rf,df->rd", hidden, down_t[i], preferred_element_type=jnp.float32)
            outs.append(down.astype(jnp.bfloat16))
        outs = jnp.concatenate(outs, 0)

    if compact:
        return combine_plane(spread, outs, tok)

    results = []
    wide = cols // TAIL_PIECES
    for c in range(TAIL_PIECES):
        term = jnp.dot(
            spread, outs[:, c * wide : (c + 1) * wide], preferred_element_type=jnp.float32
        ).astype(jnp.bfloat16).reshape(n_seq, tok, wide)
        for bit in reversed(bits_down(n_seq)):
            pairs = term.reshape(term.shape[0] // 2, 2, tok, wide)
            got = swap(pairs[:, 1], "seq", bit)
            term = (pairs[:, 0].astype(jnp.float32) + got.astype(jnp.float32)).astype(jnp.bfloat16)
        chunks = term.reshape(n_exp, tok // n_exp, wide)
        total = chunks[0].astype(jnp.float32)
        for d in range(1, n_exp):
            total = total + swap(chunks[d], "exp", d).astype(jnp.float32)
        results.append(total.astype(jnp.bfloat16))
    return jnp.concatenate(results, 1)


def solution(mesh):
    in_specs = (
        P("seq", None),
        P("seq", None),
        P("seq", None),
        P(),
        P("seq", None),
        P("seq", None),
        P("exp", "rep", None, "seq"),
        P("exp", "rep", "seq"),
    )
    out_specs = P(("seq", "exp"), "rep")
    return jax.shard_map(
        per_device, mesh=mesh, in_specs=in_specs, out_specs=out_specs, check_vma=False
    )
```
